32 devices in a mesh: rep: 2 (over x), node: 16 (over z, y, core).
Axes of the slice: x: 2, y: 2, z: 4, core: 2. Of those that a mesh axis runs over, the one named last changes fastest.
Arguments:
- tokens: bfloat16 [4096, 7168], P(('rep', 'node')), parts along dimension 0, may hold values from -6 to 6
- group_choice: int32 [4096, 4], P(('rep', 'node')), parts along dimension 0, may hold values from 0 to 7, as said below
- expert_picks: int32 [4096, 8], P(('rep', 'node')), parts along dimension 0, may hold values from 0 to 255, as said below
- gate_fixed: int32 [4096, 8], P(('rep', 'node')), parts along dimension 0, may hold values from 1 to 65535
- token_counts: int32 [32], P(('rep', 'node')), parts along dimension 0, may hold values from 16 to 128, as said below
- expert_gate: bfloat16 [7168, 2048], P(None, 'node'), may hold values from -0.0625 to 0.0625
- expert_up: bfloat16 [7168, 2048], P(None, 'node'), may hold values from -0.0625 to 0.0625
- expert_down: bfloat16 [2048, 7168], P('node'), may hold values from -0.1875 to 0.1875
Outputs:
- routed_out: bfloat16 [4096, 7168], P(('rep', 'node')), parts along dimension 0
The draws below stay inside these ranges and needn't reach their ends.
There are 2 independent parts, one for each index of `rep`. The reference program is written for one: setup_inputs(seed, part) draws one part's arguments, and reference() takes and returns one part's arrays. A program takes and returns all parts, laid end to end along the dimension named above; an argument that names none is the same for every part. Nothing has to cross between parts.
Inputs may be any that keep to these rules, and one draw needn't show every extreme that they name: `group_choice`: each row holds 4 different groups. `expert_picks`: each row names 8 different experts, two from each group of the same row of group_choice (expert e lies in group e // 32); at most one of them is a held expert f * 32 with f < 2. Among the valid tokens of one device each held expert is picked at most 8 times, and in every draw one held expert is picked exactly 8 times on every device. `token_counts`: some device has 128 valid tokens and some device 2 * 8.
All inputs are finite; a program needn't handle non-finite values.
Results may differ from the reference program's by a relative error of at most 0.0064.
Values may be sent and summed in bfloat16 or wider, within the bound.
A program may use at most 64 MiB of HBM per device.

```python
import jax
import jax.numpy as jnp

D = 7168
FFW = 1024
GROUPS = 8
TOPG = 4
TOPK = 8
SPLIT = 8
TOK_DEV = 128
GROUP_SIZE = 32
HID = 128
FLIGHT = 2
CAP = 8
TOKENS = 2048


def routing_tables(key):
    dev_count = TOKENS // TOK_DEV
    subkeys = [jax.random.fold_in(key, 7001 + number) for number in range(12)]
    base_counts = jax.random.randint(subkeys[0], (dev_count,), FLIGHT * CAP, TOK_DEV + 1)
    dev_order = jax.random.permutation(subkeys[1], dev_count)
    dev_ids = jnp.arange(dev_count)
    token_counts = jnp.where(dev_ids == dev_order[0], TOK_DEV, base_counts)
    token_counts = jnp.where(dev_ids == dev_order[1], FLIGHT * CAP, token_counts)
    heavy_caps = jax.random.randint(subkeys[2], (FLIGHT,), 1, CAP + 1)
    load_sizes = jax.random.randint(subkeys[3], (dev_count, FLIGHT), 0, 1 << 16) % heavy_caps[None, :] + 1
    chosen = jax.random.randint(subkeys[4], (), 0, FLIGHT)
    load_sizes = jnp.where(jnp.arange(FLIGHT)[None, :] == chosen, CAP, load_sizes)
    local_ids = jnp.arange(TOK_DEV)
    scores = jax.random.randint(subkeys[5], (dev_count, TOK_DEV), 0, 1 << 16) * TOK_DEV + local_ids[None, :]
    scores = scores + jnp.where(local_ids[None, :] >= token_counts[:, None], (1 << 16) * TOK_DEV, 0)
    token_rank = jnp.argsort(jnp.argsort(scores, axis=1), axis=1)
    load_ends = jnp.cumsum(load_sizes, axis=1)
    starts = load_ends - load_sizes
    inside = (token_rank[:, :, None] >= starts[:, None, :]) & (token_rank[:, :, None] < load_ends[:, None, :])
    has_flight = jnp.any(inside, axis=2)
    flight_id = jnp.sum(jnp.where(inside, jnp.arange(FLIGHT)[None, None, :], 0), axis=2)
    invalid_slot = local_ids[None, :] >= token_counts[:, None]
    extra_pick = jax.random.randint(subkeys[11], (dev_count, TOK_DEV), 0, 2 * FLIGHT)
    invalid_held = invalid_slot & (extra_pick < FLIGHT)
    has_flight = (has_flight | invalid_held).reshape(TOKENS)
    flight_id = jnp.where(invalid_held, extra_pick, flight_id).reshape(TOKENS)
    group_score = jax.random.randint(subkeys[6], (TOKENS, GROUPS), 0, 1 << 16) * GROUPS + jnp.arange(GROUPS)[None, :]
    group_score = jnp.where(has_flight[:, None] & (jnp.arange(GROUPS)[None, :] == flight_id[:, None]), -1, group_score)
    groups = jnp.argsort(group_score, axis=1)[:, :TOPG]
    first_off = jax.random.randint(subkeys[7], (TOKENS, TOPG), 1, GROUP_SIZE)
    second = 1 + (first_off - 1 + jax.random.randint(subkeys[8], (TOKENS, TOPG), 1, GROUP_SIZE - 1)) % (GROUP_SIZE - 1)
    first_off = jnp.where((jnp.arange(TOPG)[None, :] == 0) & has_flight[:, None], 0, first_off)
    picked_experts = jnp.stack([groups * GROUP_SIZE + first_off, groups * GROUP_SIZE + second], axis=2).reshape(TOKENS, TOPK)
    column_score = jax.random.randint(subkeys[9], (TOKENS, TOPK), 0, 1 << 16) * TOPK + jnp.arange(TOPK)[None, :]
    picked_experts = jnp.take_along_axis(picked_experts, jnp.argsort(column_score, axis=1), axis=1)
    group_order = jax.random.randint(subkeys[10], (TOKENS, TOPG), 0, 1 << 16) * TOPG + jnp.arange(TOPG)[None, :]
    groups = jnp.take_along_axis(groups, jnp.argsort(group_order, axis=1), axis=1)
    return (token_counts.astype(jnp.int32), groups.astype(jnp.int32), picked_experts.astype(jnp.int32))


def draw_token_counts(key, part):
    return routing_tables(key)[0]


def draw_group_choice(key, part):
    return routing_tables(key)[1]


def draw_expert_picks(key, part):
    return routing_tables(key)[2]


def plant(values, rng, low, top_value):
    index_at = [jax.random.randint(jax.random.fold_in(rng, axis), (), 0, length) for axis, length in enumerate(values.shape)]
    widest = values.shape.index(max(values.shape))
    next_to = index_at[:widest] + [(index_at[widest] + 1) % values.shape[widest]] + index_at[widest + 1:]
    return values.at[tuple(index_at)].set(low).at[tuple(next_to)].set(top_value)


def levels(rng, extent, shards, low, high):
    def one(dim, shards_of):
        steps = jax.random.uniform(jax.random.fold_in(jax.random.fold_in(rng, 6), dim), (shards_of,), jnp.float32, low / len(shards), high / len(shards))
        return jnp.repeat(jnp.exp(steps), extent[dim] // shards_of).reshape((-1,) + (1,) * (len(extent) - dim - 1))

    loudness = one(*shards[0])
    for cut in shards[1:]:
        loudness = loudness * one(*cut)
    return loudness


def bell_draw(rng, extent, width, reach, cuts=(), held_as=jnp.bfloat16):
    factor_of = levels(rng, extent, cuts, -0.22, 0.18) if cuts else 1.0
    array = jax.random.normal(rng, extent, jnp.float32) * width * factor_of
    return jnp.minimum(jnp.maximum(array, -reach), reach).astype(held_as)


def setup_inputs(seed: int = 0, part: int = 0) -> dict:
    key_of = jax.random.split(jax.random.key(seed), 9)
    part_keys = jax.random.split(jax.random.fold_in(key_of[8], part), 9)
    return {
        "tokens": bell_draw(part_keys[0], (TOKENS, D), 1.0, 6.0, ((0, 16),)),
        "group_choice": draw_group_choice(jax.random.fold_in(jax.random.fold_in(key_of[8], part), 71), part),
        "expert_picks": draw_expert_picks(jax.random.fold_in(jax.random.fold_in(key_of[8], part), 71), part),
        "gate_fixed": plant(jax.random.randint(part_keys[3], (TOKENS, TOPK), 1, 65536), jax.random.fold_in(part_keys[3], 1), 1, 65535).astype(jnp.int32),
        "token_counts": draw_token_counts(jax.random.fold_in(jax.random.fold_in(key_of[8], part), 71), part),
        "expert_gate": bell_draw(key_of[5], (D, FLIGHT * FFW), D ** -0.5, 0.0625, ((1, 16),)),
        "expert_up": bell_draw(key_of[6], (D, FLIGHT * FFW), D ** -0.5, 0.0625, ((1, 16),)),
        "expert_down": bell_draw(key_of[7], (FLIGHT * FFW, D), FFW ** -0.5, 0.1875, ((0, 16),)),
    }


def expert_output(rows_in, expert_gate, expert_up, expert_down, expert):
    total = jnp.zeros((rows_in.shape[0], expert_down.shape[1]), jnp.float32)
    for member in range(SPLIT):
        column = (expert * SPLIT + member) * HID
        gate_val = jnp.dot(rows_in, expert_gate[:, column:column + HID], preferred_element_type=jnp.float32)
        up_val = jnp.dot(rows_in, expert_up[:, column:column + HID], preferred_element_type=jnp.float32)
        hidden = (jax.nn.silu(gate_val) * up_val).astype(jnp.bfloat16)
        partial_out = jnp.dot(hidden, expert_down[column:column + HID, :], preferred_element_type=jnp.float32).astype(jnp.bfloat16)
        total = total + partial_out.astype(jnp.float32)
    return total.astype(jnp.bfloat16)


def reference(tokens, group_choice, expert_picks, gate_fixed, token_counts, expert_gate, expert_up, expert_down):
    total_rows = tokens.shape[0]
    position = jnp.arange(total_rows, dtype=jnp.int32)
    device_of = position // TOK_DEV
    is_valid = (position % TOK_DEV) < token_counts[device_of]
    gate_vals = gate_fixed.astype(jnp.float32)
    weight = 2.5 * gate_vals / jnp.sum(gate_vals, axis=1, keepdims=True)
    in_group = jnp.any((expert_picks // GROUP_SIZE)[:, :, None] == group_choice[:, None, :], axis=2)
    counted = in_group & is_valid[:, None]
    result = jnp.zeros(tokens.shape, jnp.float32)
    capacity = (total_rows // TOK_DEV) * CAP
    for expert in range(FLIGHT):
        matches = counted & (expert_picks == expert * GROUP_SIZE)
        picked = jnp.any(matches, axis=1)
        shares = jnp.sum(jnp.where(matches, weight, 0.0), axis=1)
        chosen = jnp.argsort(jnp.where(picked, 0, 1).astype(jnp.int32), stable=True)[:capacity].astype(jnp.int32)
        outputs = expert_output(tokens[chosen], expert_gate, expert_up, expert_down, expert)
        result = result.at[chosen].add(outputs.astype(jnp.float32) * shares[chosen][:, None])
    return result.astype(jnp.bfloat16)
```

```python
import functools

import jax
import jax.numpy as jnp
from jax import lax
from jax.experimental import pallas as pl
from jax.experimental.pallas import tpu as pltpu
from jax.sharding import PartitionSpec as P

SPLIT = 8
GROUP_SIZE = 32
MESH = pl.DeviceIdType.MESH
SIB, NEAR, FAR = 1, 2, 4


def kernel(
    flight,
    cap,
    tokens_hbm,
    groups_ref,
    picks_ref,
    gates_ref,
    count_ref,
    gate_hbm,
    up_hbm,
    down_hbm,
    hit_ref,
    share_ref,
    outs_ref,
    tok,
    wgate,
    wup,
    wdown,
    send_unit,
    rows,
    part,
    part_bf,
    diag_in,
    sums_in,
    home_out,
    home_in,
    tok_sem,
    own_sem,
    wsend_sem,
    wrecv_sem,
    usend_sem,
    urecv_sem,
    nsend_sem,
    fsend_sem,
    rrecv_sem,
    dsend_sem,
    drecv_sem,
    ssend_sem,
    srecv_sem,
    hsend_sem,
    hrecv_sem,
):
    me = lax.axis_index("node")
    core = lax.rem(me, 2)
    group = me // SPLIT
    member = lax.rem(me, SPLIT)
    width = tok.shape[1]
    hid = gate_hbm.shape[1]
    token_rows = tok.shape[0]

    def flipped(bit):
        return me + bit - 2 * bit * lax.rem(me // bit, 2)

    sib, near, far = flipped(SIB), flipped(NEAR), flipped(FAR)

    def peer(step):
        return lax.rem(group + step, flight) * SPLIT + member

    tok_copy = pltpu.make_async_copy(tokens_hbm, tok, tok_sem)
    tok_copy.start()

    barrier = pltpu.get_barrier_semaphore()
    partners = [sib, near, far] + [peer(step) for step in range(1, flight)]
    for partner in partners:
        pl.semaphore_signal(barrier, inc=1, device_id={"node": partner}, device_id_type=MESH)

    mine, theirs = pl.ds(0, hid), pl.ds(hid, hid)
    own_copies = [
        pltpu.make_async_copy(gate_hbm, wgate.at[:, mine], own_sem.at[0]),
        pltpu.make_async_copy(up_hbm, wup.at[:, mine], own_sem.at[1]),
        pltpu.make_async_copy(down_hbm, wdown.at[mine, :], own_sem.at[2]),
    ]
    for copy in own_copies:
        copy.start()

    valid = lax.broadcasted_iota(jnp.int32, (token_rows, 1), 0) < count_ref[0]
    gate_vals = gates_ref[...].astype(jnp.float32)
    weight = 2.5 * gate_vals / jnp.sum(gate_vals, axis=1, keepdims=True)
    picks = picks_ref[...]
    groups = groups_ref[...]
    lane = lax.broadcasted_iota(jnp.int32, (token_rows, flight * cap), 1)
    picked = jnp.zeros((token_rows, flight * cap), jnp.float32)
    share = jnp.zeros((token_rows, 1), jnp.float32)
    for step in range(flight):
        expert = lax.rem(group + step, flight)
        chosen = jnp.max((groups == expert).astype(jnp.float32), axis=1, keepdims=True)
        chosen = jnp.where(valid, chosen, 0.0)
        match = (picks == expert * GROUP_SIZE).astype(jnp.float32) * chosen
        share = share + jnp.sum(match * weight, axis=1, keepdims=True)
        here = jnp.max(match, axis=1, keepdims=True)
        in_step = (lane >= step * cap) & (lane < (step + 1) * cap)
        picked = jnp.where(in_step, here, picked)
    below = lax.broadcasted_iota(jnp.int32, (token_rows, token_rows), 0)
    above = lax.broadcasted_iota(jnp.int32, (token_rows, token_rows), 1)
    tri = (above <= below).astype(jnp.bfloat16)
    slot = jnp.dot(tri, picked.astype(jnp.bfloat16), preferred_element_type=jnp.float32) - 1.0
    want = lax.rem(lane, cap).astype(jnp.float32)
    hit = jnp.where(slot == want, picked, 0.0).astype(jnp.bfloat16)
    hit_ref[...] = hit
    share_ref[...] = share

    tok_copy.wait()
    chunk = width // 7 if width % (7 * 128) == 0 else width
    for at in range(0, width, chunk):
        cols = pl.ds(at, chunk)
        got = lax.dot_general(
            hit, tok[:, cols], (((0,), (0,)), ((), ())), preferred_element_type=jnp.float32
        ).astype(jnp.bfloat16)
        for step in range(flight):
            unit = got[step * cap : (step + 1) * cap]
            if step == 0:
                rows[0, 0, :, cols] = unit
            else:
                send_unit[step, :, cols] = unit

    pl.semaphore_wait(barrier, len(partners))

    def remote(src, dst, send_sem, recv_sem, target):
        copy = pltpu.make_async_remote_copy(
            src_ref=src,
            dst_ref=dst,
            send_sem=send_sem,
            recv_sem=recv_sem,
            device_id={"node": target},
            device_id_type=MESH,
        )
        copy.start()
        return copy

    unit_copies = [None]
    for step in range(1, flight):
        unit_copies.append(
            remote(
                send_unit.at[step],
                rows.at[flight - step, 0],
                usend_sem.at[step],
                urecv_sem.at[flight - step],
                peer(step),
            )
        )

    def spread(e):
        return [
            remote(rows.at[e, 0], rows.at[e, 1], nsend_sem.at[e, 0], rrecv_sem.at[e, 0], near),
            remote(rows.at[e, 0], rows.at[e, 2], nsend_sem.at[e, 1], rrecv_sem.at[e, 1], far),
        ]

    via = jnp.where(core == 0, near, far)
    other_via = jnp.where(core == 0, far, near)

    def arrived(dst, recv_sem):
        pltpu.make_async_copy(dst, dst, recv_sem).wait()

    def forward(e):
        src = 2 - core
        arrived(rows.at[e, src], rrecv_sem.at[e, src - 1])
        return remote(rows.at[e, src], rows.at[e, 3], fsend_sem.at[e], rrecv_sem.at[e, 2], via)

    spreads = [spread(0)]
    w_copies = [
        remote(gate_hbm, wgate.at[:, theirs], wsend_sem.at[0], wrecv_sem.at[0], sib),
        remote(up_hbm, wup.at[:, theirs], wsend_sem.at[1], wrecv_sem.at[1], sib),
        remote(down_hbm, wdown.at[theirs, :], wsend_sem.at[2], wrecv_sem.at[2], sib),
    ]
    forwards = [forward(0)]
    for e in range(1, flight):
        arrived(rows.at[e, 0], urecv_sem.at[e])
        spreads.append(spread(e))

    def rest(e):
        arrived(rows.at[e, 1 + core], rrecv_sem.at[e, core])
        arrived(rows.at[e, 3], rrecv_sem.at[e, 2])

    def hidden(low, high):
        count = (high - low) * 4 * cap
        x = rows[low:high].reshape(count, width)
        gate_val = jnp.dot(x, wgate[...], preferred_element_type=jnp.float32)
        up_val = jnp.dot(x, wup[...], preferred_element_type=jnp.float32)
        return (gate_val / (1.0 + jnp.exp(-gate_val)) * up_val).astype(jnp.bfloat16)

    def project(h, low, high):
        for at in range(0, width, chunk):
            cols = pl.ds(at, chunk)
            val = jnp.dot(h, wdown[:, cols], preferred_element_type=jnp.float32)
            val = val.reshape(high - low, 4, cap, chunk)
            part[low:high, :, :, cols] = val
            part_bf[low:high, :, :, cols] = val.astype(jnp.bfloat16)

    def send_diag(e):
        return remote(part_bf.at[e, 3], diag_in.at[e], dsend_sem.at[e], drecv_sem.at[e], other_via)

    rest(0)
    for number in range(2):
        own_copies[number].wait()
        w_copies[number].wait_recv()
    hidden_first = hidden(0, 1)
    for e in range(1, flight):
        forwards.append(forward(e))
    own_copies[2].wait()
    w_copies[2].wait_recv()
    project(hidden_first, 0, 1)
    diags = [send_diag(0)]
    if flight > 1:
        for e in range(1, flight):
            rest(e)
        project(hidden(1, flight), 1, flight)
        for e in range(1, flight):
            diags.append(send_diag(e))

    late = []
    for e in range(flight):
        arrived(diag_in.at[e], drecv_sem.at[e])
        slot_to = 1 + core
        part_bf[e, slot_to] = (part[e, slot_to] + diag_in[e].astype(jnp.float32)).astype(jnp.bfloat16)
        late.append(remote(part_bf.at[e, 1], sums_in.at[e, 0], ssend_sem.at[e, 0], srecv_sem.at[e, 0], near))
        late.append(remote(part_bf.at[e, 2], sums_in.at[e, 1], ssend_sem.at[e, 1], srecv_sem.at[e, 1], far))

    def total(e):
        for way in range(2):
            arrived(sums_in.at[e, way], srecv_sem.at[e, way])
        val = part[e, 0] + sums_in[e, 0].astype(jnp.float32) + sums_in[e, 1].astype(jnp.float32)
        return val.astype(jnp.bfloat16)

    for e in range(1, flight):
        home_out[e] = total(e)
        late.append(
            remote(home_out.at[e], home_in.at[flight - e], hsend_sem.at[e], hrecv_sem.at[flight - e], peer(e))
        )
    outs_ref[0] = total(0)
    for step in range(1, flight):
        arrived(home_in.at[step], hrecv_sem.at[step])
        outs_ref[step] = home_in[step]

    for copy in (
        [c for c in unit_copies if c is not None]
        + [c for pair in spreads for c in pair]
        + forwards
        + w_copies
        + diags
        + late
    ):
        copy.wait_send()


def local(
    tokens,
    group_choice,
    expert_picks,
    gate_fixed,
    token_counts,
    expert_gate,
    expert_up,
    expert_down,
):
    flight = lax.axis_size("node") // SPLIT
    token_rows, width = tokens.shape
    cap = token_rows // 16
    hid = expert_gate.shape[1]
    vmem = pl.BlockSpec(memory_space=pltpu.VMEM)
    anywhere = pl.BlockSpec(memory_space=pl.ANY)
    dma = pltpu.SemaphoreType.DMA
    hit, share, outs = pl.pallas_call(
        functools.partial(kernel, flight, cap),
        out_shape=(
            jax.ShapeDtypeStruct((token_rows, flight * cap), jnp.bfloat16),
            jax.ShapeDtypeStruct((token_rows, 1), jnp.float32),
            jax.ShapeDtypeStruct((flight, cap, width), jnp.bfloat16),
        ),
        in_specs=[
            anywhere,
            vmem,
            vmem,
            vmem,
            pl.BlockSpec(memory_space=pltpu.SMEM),
            anywhere,
            anywhere,
            anywhere,
        ],
        out_specs=(vmem, vmem, vmem),
        scratch_shapes=[
            pltpu.VMEM((token_rows, width), jnp.bfloat16),
            pltpu.VMEM((width, 2 * hid), jnp.bfloat16),
            pltpu.VMEM((width, 2 * hid), jnp.bfloat16),
            pltpu.VMEM((2 * hid, width), jnp.bfloat16),
            pltpu.VMEM((flight, cap, width), jnp.bfloat16),
            pltpu.VMEM((flight, 4, cap, width), jnp.bfloat16),
            pltpu.VMEM((flight, 4, cap, width), jnp.float32),
            pltpu.VMEM((flight, 4, cap, width), jnp.bfloat16),
            pltpu.VMEM((flight, cap, width), jnp.bfloat16),
            pltpu.VMEM((flight, 2, cap, width), jnp.bfloat16),
            pltpu.VMEM((flight, cap, width), jnp.bfloat16),
            pltpu.VMEM((flight, cap, width), jnp.bfloat16),
            dma(()),
            dma((3,)),
            dma((3,)),
            dma((3,)),
            dma((flight,)),
            dma((flight,)),
            dma((flight, 2)),
            dma((flight,)),
            dma((flight, 3)),
            dma((flight,)),
            dma((flight,)),
            dma((flight, 2)),
            dma((flight, 2)),
            dma((flight,)),
            dma((flight,)),
        ],
        compiler_params=pltpu.CompilerParams(
            collective_id=0, has_side_effects=True, vmem_limit_bytes=56 * 1024 * 1024
        ),
    )(tokens, group_choice, expert_picks, gate_fixed, token_counts, expert_gate, expert_up, expert_down)
    back = jnp.dot(hit, outs.reshape(flight * cap, width), preferred_element_type=jnp.float32)
    return (back * share).astype(jnp.bfloat16)


def solution(mesh):
    return jax.shard_map(
        local,
        mesh=mesh,
        in_specs=(
            P(("rep", "node"), None),
            P(("rep", "node"), None),
            P(("rep", "node"), None),
            P(("rep", "node"), None),
            P(("rep", "node")),
            P(None, "node"),
            P(None, "node"),
            P("node", None),
        ),
        out_specs=P(("rep", "node"), None),
        check_vma=False,
    )
```

```python
import functools

import jax
import jax.numpy as jnp
from jax import lax
from jax.experimental import pallas as pl
from jax.experimental.pallas import tpu as pltpu
from jax.sharding import PartitionSpec as P

SPLIT = 8
GROUP_SIZE = 32
MESH = pl.DeviceIdType.MESH
SIB, NEAR, FAR = 1, 2, 4


def kernel(
    flight,
    cap,
    tokens_hbm,
    groups_ref,
    picks_ref,
    gates_ref,
    count_ref,
    gate_hbm,
    up_hbm,
    down_hbm,
    hit_ref,
    share_ref,
    outs_ref,
    tok,
    wgate,
    wup,
    wdown,
    send_unit,
    rows,
    part,
    part_bf,
    diag_in,
    sums_in,
    home_out,
    home_in,
    tok_sem,
    own_sem,
    wsend_sem,
    wrecv_sem,
    usend_sem,
    urecv_sem,
    nsend_sem,
    rrecv_sem,
    dsend_sem,
    drecv_sem,
    ssend_sem,
    srecv_sem,
    hsend_sem,
    hrecv_sem,
):
    me = lax.axis_index("node")
    group = me // SPLIT
    member = lax.rem(me, SPLIT)
    width = tok.shape[1]
    hid = gate_hbm.shape[1]
    token_rows = tok.shape[0]

    def flipped(bit):
        return me + bit - 2 * bit * lax.rem(me // bit, 2)

    sib, near, far = flipped(SIB), flipped(NEAR), flipped(FAR)

    def peer(step):
        return lax.rem(group + step, flight) * SPLIT + member

    tok_copy = pltpu.make_async_copy(tokens_hbm, tok, tok_sem)
    tok_copy.start()

    barrier = pltpu.get_barrier_semaphore()
    partners = [sib, near, far] + [peer(step) for step in range(1, flight)]
    for partner in partners:
        pl.semaphore_signal(barrier, inc=1, device_id={"node": partner}, device_id_type=MESH)

    mine, theirs = pl.ds(0, hid), pl.ds(hid, hid)
    own_copies = [
        pltpu.make_async_copy(gate_hbm, wgate.at[:, mine], own_sem.at[0]),
        pltpu.make_async_copy(up_hbm, wup.at[:, mine], own_sem.at[1]),
        pltpu.make_async_copy(down_hbm, wdown.at[mine, :], own_sem.at[2]),
    ]
    for copy in own_copies:
        copy.start()

    valid = lax.broadcasted_iota(jnp.int32, (1, token_rows), 1) < count_ref[0]
    gate_vals = gates_ref[...].astype(jnp.float32)
    weight = 2.5 * gate_vals / jnp.sum(gate_vals, axis=0, keepdims=True)
    picks = picks_ref[...]
    groups = groups_ref[...]
    place = lax.broadcasted_iota(jnp.int32, (flight * cap, token_rows), 0)
    picked = jnp.zeros((flight * cap, token_rows), jnp.float32)
    share = jnp.zeros((1, token_rows), jnp.float32)
    for step in range(flight):
        expert = lax.rem(group + step, flight)
        chosen = jnp.max((groups == expert).astype(jnp.float32), axis=0, keepdims=True)
        chosen = jnp.where(valid, chosen, 0.0)
        match = (picks == expert * GROUP_SIZE).astype(jnp.float32) * chosen
        share = share + jnp.sum(match * weight, axis=0, keepdims=True)
        here = jnp.max(match, axis=0, keepdims=True)
        in_step = (place >= step * cap) & (place < (step + 1) * cap)
        picked = jnp.where(in_step, here, picked)
    down_id = lax.broadcasted_iota(jnp.int32, (token_rows, token_rows), 0)
    right_id = lax.broadcasted_iota(jnp.int32, (token_rows, token_rows), 1)
    tri = (down_id <= right_id).astype(jnp.bfloat16)
    slot = jnp.dot(picked.astype(jnp.bfloat16), tri, preferred_element_type=jnp.float32) - 1.0
    want = lax.rem(place, cap).astype(jnp.float32)
    hit = jnp.where(slot == want, picked, 0.0).astype(jnp.bfloat16)
    hit_ref[...] = hit

    def remote(src, dst, send_sem, recv_sem, target):
        copy = pltpu.make_async_remote_copy(
            src_ref=src,
            dst_ref=dst,
            send_sem=send_sem,
            recv_sem=recv_sem,
            device_id={"node": target},
            device_id_type=MESH,
        )
        copy.start()
        return copy

    def arrived(dst, recv_sem):
        pltpu.make_async_copy(dst, dst, recv_sem).wait()

    pl.semaphore_wait(barrier, len(partners))
    w_copies = [
        remote(gate_hbm, wgate.at[:, theirs], wsend_sem.at[0], wrecv_sem.at[0], sib),
        remote(up_hbm, wup.at[:, theirs], wsend_sem.at[1], wrecv_sem.at[1], sib),
        remote(down_hbm, wdown.at[theirs, :], wsend_sem.at[2], wrecv_sem.at[2], sib),
    ]

    tok_copy.wait()
    chunk = width // 7 if width % (7 * 128) == 0 else width
    for at in range(0, width, chunk):
        cols = pl.ds(at, chunk)
        got = jnp.dot(hit, tok[:, cols], preferred_element_type=jnp.float32).astype(jnp.bfloat16)
        for step in range(flight):
            unit = got[step * cap : (step + 1) * cap]
            if step == 0:
                rows[0, 0, :, cols] = unit
            else:
                send_unit[step, :, cols] = unit

    cut = width // 128 * 3 // 4 * 128
    spans = (pl.ds(0, cut), pl.ds(cut, width - cut))
    LO, HI = 0, 1
    sent = []

    for step in range(1, flight):
        for half in (HI, LO):
            sent.append(
                remote(
                    send_unit.at[step, :, spans[half]],
                    rows.at[flight - step, 0, :, spans[half]],
                    usend_sem.at[step, half],
                    urecv_sem.at[flight - step, half],
                    peer(step),
                )
            )

    def pass_on(e, src, dst, half, target):
        number = 2 * (dst - 1) + half
        sent.append(
            remote(
                rows.at[e, src, :, spans[half]],
                rows.at[e, dst, :, spans[half]],
                nsend_sem.at[e, number],
                rrecv_sem.at[e, number],
                target,
            )
        )

    def got_rows(e, src, half):
        arrived(rows.at[e, src, :, spans[half]], rrecv_sem.at[e, 2 * (src - 1) + half])

    def spread(e, half):
        if half == HI:
            pass_on(e, 0, 1, half, near)
            pass_on(e, 0, 2, half, far)
        else:
            pass_on(e, 0, 2, half, far)
            pass_on(e, 0, 1, half, near)

    def forward(e):
        got_rows(e, 1, HI)
        pass_on(e, 1, 3, HI, far)
        got_rows(e, 2, LO)
        pass_on(e, 2, 3, LO, near)

    spread(0, HI)
    spread(0, LO)
    share_ref[...] = jnp.sum(jnp.where(down_id == right_id, share, 0.0), axis=1, keepdims=True)
    forward(0)
    for half in (HI, LO):
        for e in range(1, flight):
            arrived(rows.at[e, 0, :, spans[half]], urecv_sem.at[e, half])
            spread(e, half)

    def rest(e):
        got_rows(e, 1, LO)
        got_rows(e, 2, HI)
        got_rows(e, 3, HI)
        got_rows(e, 3, LO)

    def hidden(low, high):
        count = (high - low) * 4 * cap
        x = rows[low:high].reshape(count, width)
        gate_val = jnp.dot(x, wgate[...], preferred_element_type=jnp.float32)
        up_val = jnp.dot(x, wup[...], preferred_element_type=jnp.float32)
        return (gate_val / (1.0 + jnp.exp(-gate_val)) * up_val).astype(jnp.bfloat16)

    def project(h, low, high):
        for at in range(0, width, chunk):
            cols = pl.ds(at, chunk)
            val = jnp.dot(h, wdown[:, cols], preferred_element_type=jnp.float32)
            val = val.reshape(high - low, 4, cap, chunk)
            part[low:high, :, :, cols] = val
            part_bf[low:high, :, :, cols] = val.astype(jnp.bfloat16)

    def send_diag(e, half):
        sent.append(
            remote(
                part_bf.at[e, 3, :, spans[half]],
                diag_in.at[e, :, spans[half]],
                dsend_sem.at[e, half],
                drecv_sem.at[e, half],
                near if half == LO else far,
            )
        )

    def send_sum(e, way, half):
        number = 2 * way + half
        sent.append(
            remote(
                part_bf.at[e, 1 + way, :, spans[half]],
                sums_in.at[e, way, :, spans[half]],
                ssend_sem.at[e, number],
                srecv_sem.at[e, number],
                far if way else near,
            )
        )

    def give_back(e):
        send_diag(e, HI)
        send_diag(e, LO)
        send_sum(e, 1, HI)
        send_sum(e, 0, LO)

    rest(0)
    for number in range(2):
        own_copies[number].wait()
        w_copies[number].wait_recv()
    hidden_first = hidden(0, 1)
    for e in range(1, flight):
        forward(e)
    own_copies[2].wait()
    w_copies[2].wait_recv()
    project(hidden_first, 0, 1)
    give_back(0)
    if flight > 1:
        for e in range(1, flight):
            rest(e)
        project(hidden(1, flight), 1, flight)
        for e in range(1, flight):
            give_back(e)

    for e in range(flight):
        for half, way in ((HI, 0), (LO, 1)):
            cols = spans[half]
            arrived(diag_in.at[e, :, cols], drecv_sem.at[e, half])
            val = part[e, 1 + way, :, cols] + diag_in[e, :, cols].astype(jnp.float32)
            part_bf[e, 1 + way, :, cols] = val.astype(jnp.bfloat16)
            send_sum(e, way, half)

    def total(e, half):
        cols = spans[half]
        for way in range(2):
            arrived(sums_in.at[e, way, :, cols], srecv_sem.at[e, 2 * way + half])
        val = part[e, 0, :, cols] + sums_in[e, 0, :, cols].astype(jnp.float32)
        val = val + sums_in[e, 1, :, cols].astype(jnp.float32)
        return val.astype(jnp.bfloat16)

    for e in range(1, flight):
        for half in (HI, LO):
            cols = spans[half]
            home_out[e, :, cols] = total(e, half)
            sent.append(
                remote(
                    home_out.at[e, :, cols],
                    home_in.at[flight - e, :, cols],
                    hsend_sem.at[e, half],
                    hrecv_sem.at[flight - e, half],
                    peer(e),
                )
            )
    for half in (HI, LO):
        outs_ref[0, :, spans[half]] = total(0, half)
    for step in range(1, flight):
        for half in (HI, LO):
            arrived(home_in.at[step, :, spans[half]], hrecv_sem.at[step, half])
        outs_ref[step] = home_in[step]

    for copy in sent + w_copies:
        copy.wait_send()


def combine(hit_ref, share_ref, outs_ref, routed_ref):
    back = lax.dot_general(
        hit_ref[...], outs_ref[...], (((0,), (0,)), ((), ())), preferred_element_type=jnp.float32
    )
    routed_ref[...] = (back * share_ref[...]).astype(routed_ref.dtype)


def local(
    tokens,
    group_choice,
    expert_picks,
    gate_fixed,
    token_counts,
    expert_gate,
    expert_up,
    expert_down,
):
    flight = lax.axis_size("node") // SPLIT
    token_rows, width = tokens.shape
    cap = token_rows // 16
    hid = expert_gate.shape[1]
    vmem = pl.BlockSpec(memory_space=pltpu.VMEM)
    anywhere = pl.BlockSpec(memory_space=pl.ANY)
    dma = pltpu.SemaphoreType.DMA
    hit, share, outs = pl.pallas_call(
        functools.partial(kernel, flight, cap),
        out_shape=(
            jax.ShapeDtypeStruct((flight * cap, token_rows), jnp.bfloat16),
            jax.ShapeDtypeStruct((token_rows, 1), jnp.float32),
            jax.ShapeDtypeStruct((flight, cap, width), jnp.bfloat16),
        ),
        in_specs=[
            anywhere,
            vmem,
            vmem,
            vmem,
            pl.BlockSpec(memory_space=pltpu.SMEM),
            anywhere,
            anywhere,
            anywhere,
        ],
        out_specs=(vmem, vmem, vmem),
        scratch_shapes=[
            pltpu.VMEM((token_rows, width), jnp.bfloat16),
            pltpu.VMEM((width, 2 * hid), jnp.bfloat16),
            pltpu.VMEM((width, 2 * hid), jnp.bfloat16),
            pltpu.VMEM((2 * hid, width), jnp.bfloat16),
            pltpu.VMEM((flight, cap, width), jnp.bfloat16),
            pltpu.VMEM((flight, 4, cap, width), jnp.bfloat16),
            pltpu.VMEM((flight, 4, cap, width), jnp.float32),
            pltpu.VMEM((flight, 4, cap, width), jnp.bfloat16),
            pltpu.VMEM((flight, cap, width), jnp.bfloat16),
            pltpu.VMEM((flight, 2, cap, width), jnp.bfloat16),
            pltpu.VMEM((flight, cap, width), jnp.bfloat16),
            pltpu.VMEM((flight, cap, width), jnp.bfloat16),
            dma(()),
            dma((3,)),
            dma((3,)),
            dma((3,)),
            dma((flight, 2)),
            dma((flight, 2)),
            dma((flight, 6)),
            dma((flight, 6)),
            dma((flight, 2)),
            dma((flight, 2)),
            dma((flight, 4)),
            dma((flight, 4)),
            dma((flight, 2)),
            dma((flight, 2)),
        ],
        compiler_params=pltpu.CompilerParams(
            collective_id=0, has_side_effects=True, vmem_limit_bytes=56 * 1024 * 1024
        ),
    )(tokens, group_choice.T, expert_picks.T, gate_fixed.T, token_counts, expert_gate, expert_up, expert_down)
    block = width // 4 if width % 512 == 0 else width
    return pl.pallas_call(
        combine,
        grid=(width // block,),
        out_shape=jax.ShapeDtypeStruct((token_rows, width), tokens.dtype),
        in_specs=[
            pl.BlockSpec((flight * cap, token_rows), lambda i: (0, 0)),
            pl.BlockSpec((token_rows, 1), lambda i: (0, 0)),
            pl.BlockSpec((flight * cap, block), lambda i: (0, i)),
        ],
        out_specs=pl.BlockSpec((token_rows, block), lambda i: (0, i)),
    )(hit, share, outs.reshape(flight * cap, width))


def solution(mesh):
    return jax.shard_map(
        local,
        mesh=mesh,
        in_specs=(
            P(("rep", "node"), None),
            P(("rep", "node"), None),
            P(("rep", "node"), None),
            P(("rep", "node"), None),
            P(("rep", "node")),
            P(None, "node"),
            P(None, "node"),
            P("node", None),
        ),
        out_specs=P(("rep", "node"), None),
        check_vma=False,
    )
```

```python
import functools

import jax
import jax.numpy as jnp
from jax import lax
from jax.experimental import pallas as pl
from jax.experimental.pallas import tpu as pltpu
from jax.sharding import PartitionSpec as P

SPLIT = 8
GROUP_SIZE = 32
MESH = pl.DeviceIdType.MESH
SIB, NEAR, FAR = 1, 2, 4


def kernel(
    flight,
    cap,
    tokens_hbm,
    groups_ref,
    picks_ref,
    gates_ref,
    count_ref,
    gate_hbm,
    up_hbm,
    down_hbm,
    hit_ref,
    share_ref,
    outs_ref,
    tok,
    wgate,
    wup,
    wdown,
    send_unit,
    rows,
    part,
    part_bf,
    diag_in,
    sums_in,
    home_out,
    home_in,
    tok_sem,
    own_sem,
    wsend_sem,
    wrecv_sem,
    usend_sem,
    urecv_sem,
    nsend_sem,
    rrecv_sem,
    dsend_sem,
    drecv_sem,
    ssend_sem,
    srecv_sem,
    hsend_sem,
    hrecv_sem,
):
    me = lax.axis_index("node")
    group = me // SPLIT
    member = lax.rem(me, SPLIT)
    width = tok.shape[1]
    hid = gate_hbm.shape[1]
    token_rows = tok.shape[0]

    def flipped(bit):
        return me + bit - 2 * bit * lax.rem(me // bit, 2)

    sib, near, far = flipped(SIB), flipped(NEAR), flipped(FAR)

    def peer(step):
        return lax.rem(group + step, flight) * SPLIT + member

    tok_copy = pltpu.make_async_copy(tokens_hbm, tok, tok_sem)
    tok_copy.start()

    barrier = pltpu.get_barrier_semaphore()
    partners = [sib, near, far] + [peer(step) for step in range(1, flight)]
    for partner in partners:
        pl.semaphore_signal(barrier, inc=1, device_id={"node": partner}, device_id_type=MESH)

    mine, theirs = pl.ds(0, hid), pl.ds(hid, hid)
    own_copies = [
        pltpu.make_async_copy(gate_hbm, wgate.at[:, mine], own_sem.at[0]),
        pltpu.make_async_copy(up_hbm, wup.at[:, mine], own_sem.at[1]),
        pltpu.make_async_copy(down_hbm, wdown.at[mine, :], own_sem.at[2]),
    ]
    valid = lax.broadcasted_iota(jnp.int32, (1, token_rows), 1) < count_ref[0]
    gate_vals = gates_ref[...].astype(jnp.float32)
    weight = 2.5 * gate_vals / jnp.sum(gate_vals, axis=0, keepdims=True)
    picks = picks_ref[...]
    groups = groups_ref[...]
    place = lax.broadcasted_iota(jnp.int32, (flight * cap, token_rows), 0)
    picked = jnp.zeros((flight * cap, token_rows), jnp.float32)
    share = jnp.zeros((1, token_rows), jnp.float32)
    for step in range(flight):
        expert = lax.rem(group + step, flight)
        chosen = jnp.max((groups == expert).astype(jnp.float32), axis=0, keepdims=True)
        chosen = jnp.where(valid, chosen, 0.0)
        match = (picks == expert * GROUP_SIZE).astype(jnp.float32) * chosen
        share = share + jnp.sum(match * weight, axis=0, keepdims=True)
        here = jnp.max(match, axis=0, keepdims=True)
        in_step = (place >= step * cap) & (place < (step + 1) * cap)
        picked = jnp.where(in_step, here, picked)
    down_id = lax.broadcasted_iota(jnp.int32, (token_rows, token_rows), 0)
    right_id = lax.broadcasted_iota(jnp.int32, (token_rows, token_rows), 1)
    tri = (down_id <= right_id).astype(jnp.bfloat16)
    slot = jnp.dot(picked.astype(jnp.bfloat16), tri, preferred_element_type=jnp.float32) - 1.0
    want = lax.rem(place, cap).astype(jnp.float32)
    hit = jnp.where(slot == want, picked, 0.0).astype(jnp.bfloat16)
    hit_ref[...] = hit
    share_ref[...] = share

    def remote(src, dst, send_sem, recv_sem, target):
        copy = pltpu.make_async_remote_copy(
            src_ref=src,
            dst_ref=dst,
            send_sem=send_sem,
            recv_sem=recv_sem,
            device_id={"node": target},
            device_id_type=MESH,
        )
        copy.start()
        return copy

    def arrived(dst, recv_sem):
        pltpu.make_async_copy(dst, dst, recv_sem).wait()

    pl.semaphore_wait(barrier, len(partners))

    cut = width // 128 * 3 // 4 * 128
    spans = (pl.ds(0, cut), pl.ds(cut, width - cut))
    LO, HI = 0, 1
    sent = []

    def send_units(half):
        for step in range(1, flight):
            sent.append(
                remote(
                    send_unit.at[step, :, spans[half]],
                    rows.at[flight - step, 0, :, spans[half]],
                    usend_sem.at[step, half],
                    urecv_sem.at[flight - step, half],
                    peer(step),
                )
            )

    def pass_on(e, src, dst, half, target):
        number = 2 * (dst - 1) + half
        sent.append(
            remote(
                rows.at[e, src, :, spans[half]],
                rows.at[e, dst, :, spans[half]],
                nsend_sem.at[e, number],
                rrecv_sem.at[e, number],
                target,
            )
        )

    def got_rows(e, src, half):
        arrived(rows.at[e, src, :, spans[half]], rrecv_sem.at[e, 2 * (src - 1) + half])

    def spread(e, half):
        if half == HI:
            pass_on(e, 0, 1, half, near)
            pass_on(e, 0, 2, half, far)
        else:
            pass_on(e, 0, 2, half, far)
            pass_on(e, 0, 1, half, near)

    def forward(e):
        got_rows(e, 1, HI)
        pass_on(e, 1, 3, HI, far)
        got_rows(e, 2, LO)
        pass_on(e, 2, 3, LO, near)

    def pieces(half):
        low, high = (0, cut) if half == LO else (cut, width)
        step = 6 * 128
        return [pl.ds(at, min(step, high - at)) for at in range(low, high, step)]

    tok_copy.wait()
    for half in (HI, LO):
        for cols in pieces(half):
            got = jnp.dot(hit, tok[:, cols], preferred_element_type=jnp.float32).astype(jnp.bfloat16)
            for step in range(flight):
                unit = got[step * cap : (step + 1) * cap]
                if step == 0:
                    rows[0, 0, :, cols] = unit
                else:
                    send_unit[step, :, cols] = unit
        send_units(half)
        spread(0, half)
    for copy in own_copies:
        copy.start()
    w_copies = [
        remote(gate_hbm, wgate.at[:, theirs], wsend_sem.at[0], wrecv_sem.at[0], sib),
        remote(up_hbm, wup.at[:, theirs], wsend_sem.at[1], wrecv_sem.at[1], sib),
        remote(down_hbm, wdown.at[theirs, :], wsend_sem.at[2], wrecv_sem.at[2], sib),
    ]
    forward(0)
    for half in (HI, LO):
        for e in range(1, flight):
            arrived(rows.at[e, 0, :, spans[half]], urecv_sem.at[e, half])
            spread(e, half)

    def rest(e):
        got_rows(e, 1, LO)
        got_rows(e, 2, HI)
        got_rows(e, 3, HI)
        got_rows(e, 3, LO)

    def hidden(low, high):
        count = (high - low) * 4 * cap
        x = rows[low:high].reshape(count, width)
        gate_val = jnp.dot(x, wgate[...], preferred_element_type=jnp.float32)
        up_val = jnp.dot(x, wup[...], preferred_element_type=jnp.float32)
        return (gate_val / (1.0 + jnp.exp(-gate_val)) * up_val).astype(jnp.bfloat16)

    def send_diag(e, half):
        sent.append(
            remote(
                part_bf.at[e, 3, :, spans[half]],
                diag_in.at[e, :, spans[half]],
                dsend_sem.at[e, half],
                drecv_sem.at[e, half],
                near if half == LO else far,
            )
        )

    def send_sum(e, way, half):
        number = 2 * way + half
        sent.append(
            remote(
                part_bf.at[e, 1 + way, :, spans[half]],
                sums_in.at[e, way, :, spans[half]],
                ssend_sem.at[e, number],
                srecv_sem.at[e, number],
                far if way else near,
            )
        )

    def project(h, low, high):
        for half in (LO, HI):
            for cols in pieces(half):
                val = jnp.dot(h, wdown[:, cols], preferred_element_type=jnp.float32)
                val = val.reshape(high - low, 4, cap, cols.size)
                part[low:high, :, :, cols] = val
                part_bf[low:high, :, :, cols] = val.astype(jnp.bfloat16)
            for e in range(low, high):
                send_diag(e, half)
                send_sum(e, 0 if half == LO else 1, half)

    rest(0)
    for number in range(2):
        own_copies[number].wait()
        w_copies[number].wait_recv()
    hidden_first = hidden(0, 1)
    for e in range(1, flight):
        forward(e)
    own_copies[2].wait()
    w_copies[2].wait_recv()
    project(hidden_first, 0, 1)
    if flight > 1:
        for e in range(1, flight):
            rest(e)
        project(hidden(1, flight), 1, flight)

    for e in range(flight):
        for half, way in ((HI, 0), (LO, 1)):
            cols = spans[half]
            arrived(diag_in.at[e, :, cols], drecv_sem.at[e, half])
            val = part[e, 1 + way, :, cols] + diag_in[e, :, cols].astype(jnp.float32)
            part_bf[e, 1 + way, :, cols] = val.astype(jnp.bfloat16)
            send_sum(e, way, half)

    def total(e, half):
        cols = spans[half]
        for way in range(2):
            arrived(sums_in.at[e, way, :, cols], srecv_sem.at[e, 2 * way + half])
        val = part[e, 0, :, cols] + sums_in[e, 0, :, cols].astype(jnp.float32)
        val = val + sums_in[e, 1, :, cols].astype(jnp.float32)
        return val.astype(jnp.bfloat16)

    for e in range(1, flight):
        for half in (HI, LO):
            cols = spans[half]
            home_out[e, :, cols] = total(e, half)
            sent.append(
                remote(
                    home_out.at[e, :, cols],
                    home_in.at[flight - e, :, cols],
                    hsend_sem.at[e, half],
                    hrecv_sem.at[flight - e, half],
                    peer(e),
                )
            )
    for half in (HI, LO):
        outs_ref[0, :, spans[half]] = total(0, half)
    for step in range(1, flight):
        for half in (HI, LO):
            arrived(home_in.at[step, :, spans[half]], hrecv_sem.at[step, half])
        outs_ref[step] = home_in[step]

    for copy in sent + w_copies:
        copy.wait_send()


def local(
    tokens,
    group_choice,
    expert_picks,
    gate_fixed,
    token_counts,
    expert_gate,
    expert_up,
    expert_down,
):
    flight = lax.axis_size("node") // SPLIT
    token_rows, width = tokens.shape
    cap = token_rows // 16
    hid = expert_gate.shape[1]
    vmem = pl.BlockSpec(memory_space=pltpu.VMEM)
    anywhere = pl.BlockSpec(memory_space=pl.ANY)
    dma = pltpu.SemaphoreType.DMA
    hit, share, outs = pl.pallas_call(
        functools.partial(kernel, flight, cap),
        out_shape=(
            jax.ShapeDtypeStruct((flight * cap, token_rows), jnp.bfloat16),
            jax.ShapeDtypeStruct((1, token_rows), jnp.float32),
            jax.ShapeDtypeStruct((flight, cap, width), jnp.bfloat16),
        ),
        in_specs=[
            anywhere,
            vmem,
            vmem,
            vmem,
            pl.BlockSpec(memory_space=pltpu.SMEM),
            anywhere,
            anywhere,
            anywhere,
        ],
        out_specs=(vmem, vmem, vmem),
        scratch_shapes=[
            pltpu.VMEM((token_rows, width), jnp.bfloat16),
            pltpu.VMEM((width, 2 * hid), jnp.bfloat16),
            pltpu.VMEM((width, 2 * hid), jnp.bfloat16),
            pltpu.VMEM((2 * hid, width), jnp.bfloat16),
            pltpu.VMEM((flight, cap, width), jnp.bfloat16),
            pltpu.VMEM((flight, 4, cap, width), jnp.bfloat16),
            pltpu.VMEM((flight, 4, cap, width), jnp.float32),
            pltpu.VMEM((flight, 4, cap, width), jnp.bfloat16),
            pltpu.VMEM((flight, cap, width), jnp.bfloat16),
            pltpu.VMEM((flight, 2, cap, width), jnp.bfloat16),
            pltpu.VMEM((flight, cap, width), jnp.bfloat16),
            pltpu.VMEM((flight, cap, width), jnp.bfloat16),
            dma(()),
            dma((3,)),
            dma((3,)),
            dma((3,)),
            dma((flight, 2)),
            dma((flight, 2)),
            dma((flight, 6)),
            dma((flight, 6)),
            dma((flight, 2)),
            dma((flight, 2)),
            dma((flight, 4)),
            dma((flight, 4)),
            dma((flight, 2)),
            dma((flight, 2)),
        ],
        compiler_params=pltpu.CompilerParams(
            collective_id=0, has_side_effects=True, vmem_limit_bytes=56 * 1024 * 1024
        ),
    )(tokens, group_choice.T, expert_picks.T, gate_fixed.T, token_counts, expert_gate, expert_up, expert_down)
    back = lax.dot_general(
        hit,
        outs.reshape(flight * cap, width),
        (((0,), (0,)), ((), ())),
        preferred_element_type=jnp.float32,
    )
    return (back * share.reshape(token_rows)[:, None]).astype(tokens.dtype)


def solution(mesh):
    return jax.shard_map(
        local,
        mesh=mesh,
        in_specs=(
            P(("rep", "node"), None),
            P(("rep", "node"), None),
            P(("rep", "node"), None),
            P(("rep", "node"), None),
            P(("rep", "node")),
            P(None, "node"),
            P(None, "node"),
            P("node", None),
        ),
        out_specs=P(("rep", "node"), None),
        check_vma=False,
    )
```

```python
import functools

import jax
import jax.numpy as jnp
from jax import lax
from jax.experimental import pallas as pl
from jax.experimental.pallas import tpu as pltpu
from jax.sharding import PartitionSpec as P

SPLIT = 8
GROUP_SIZE = 32
MESH = pl.DeviceIdType.MESH
SIB, NEAR, FAR = 1, 2, 4


def kernel(
    flight,
    cap,
    tokens_hbm,
    groups_ref,
    picks_ref,
    gates_ref,
    count_ref,
    gate_hbm,
    up_hbm,
    down_hbm,
    hit_ref,
    share_ref,
    outs_ref,
    tok,
    wgate,
    wup,
    wdown,
    send_unit,
    rows,
    part,
    part_bf,
    diag_in,
    sums_in,
    home_out,
    home_in,
    tok_sem,
    own_sem,
    wsend_sem,
    wrecv_sem,
    usend_sem,
    urecv_sem,
    nsend_sem,
    rrecv_sem,
    dsend_sem,
    drecv_sem,
    ssend_sem,
    srecv_sem,
    hsend_sem,
    hrecv_sem,
):
    me = lax.axis_index("node")
    group = me // SPLIT
    member = lax.rem(me, SPLIT)
    width = tok.shape[1]
    hid = gate_hbm.shape[1]
    token_rows = tok.shape[0]

    def flipped(bit):
        return me + bit - 2 * bit * lax.rem(me // bit, 2)

    sib, near, far = flipped(SIB), flipped(NEAR), flipped(FAR)

    def peer(step):
        return lax.rem(group + step, flight) * SPLIT + member

    tok_copy = pltpu.make_async_copy(tokens_hbm, tok, tok_sem)
    tok_copy.start()

    barrier = pltpu.get_barrier_semaphore()
    partners = [sib, near, far] + [peer(step) for step in range(1, flight)]
    for partner in partners:
        pl.semaphore_signal(barrier, inc=1, device_id={"node": partner}, device_id_type=MESH)

    mine, theirs = pl.ds(0, hid), pl.ds(hid, hid)
    own_copies = [
        pltpu.make_async_copy(gate_hbm, wgate.at[:, mine], own_sem.at[0]),
        pltpu.make_async_copy(up_hbm, wup.at[:, mine], own_sem.at[1]),
        pltpu.make_async_copy(down_hbm, wdown.at[mine, :], own_sem.at[2]),
    ]
    for copy in own_copies:
        copy.start()

    valid = lax.broadcasted_iota(jnp.int32, (1, token_rows), 1) < count_ref[0]
    gate_vals = gates_ref[...].astype(jnp.float32)
    weight = 2.5 * gate_vals / jnp.sum(gate_vals, axis=0, keepdims=True)
    picks = picks_ref[...]
    groups = groups_ref[...]
    place = lax.broadcasted_iota(jnp.int32, (flight * cap, token_rows), 0)
    picked = jnp.zeros((flight * cap, token_rows), jnp.float32)
    share = jnp.zeros((1, token_rows), jnp.float32)
    for step in range(flight):
        expert = lax.rem(group + step, flight)
        chosen = jnp.max((groups == expert).astype(jnp.float32), axis=0, keepdims=True)
        chosen = jnp.where(valid, chosen, 0.0)
        match = (picks == expert * GROUP_SIZE).astype(jnp.float32) * chosen
        share = share + jnp.sum(match * weight, axis=0, keepdims=True)
        here = jnp.max(match, axis=0, keepdims=True)
        in_step = (place >= step * cap) & (place < (step + 1) * cap)
        picked = jnp.where(in_step, here, picked)
    down_id = lax.broadcasted_iota(jnp.int32, (token_rows, token_rows), 0)
    right_id = lax.broadcasted_iota(jnp.int32, (token_rows, token_rows), 1)
    tri = (down_id <= right_id).astype(jnp.bfloat16)
    slot = jnp.dot(picked.astype(jnp.bfloat16), tri, preferred_element_type=jnp.float32) - 1.0
    want = lax.rem(place, cap).astype(jnp.float32)
    hit = jnp.where(slot == want, picked, 0.0).astype(jnp.bfloat16)
    hit_ref[...] = hit
    share_ref[...] = share

    def remote(src, dst, send_sem, recv_sem, target):
        copy = pltpu.make_async_remote_copy(
            src_ref=src,
            dst_ref=dst,
            send_sem=send_sem,
            recv_sem=recv_sem,
            device_id={"node": target},
            device_id_type=MESH,
        )
        copy.start()
        return copy

    def arrived(dst, recv_sem):
        pltpu.make_async_copy(dst, dst, recv_sem).wait()

    pl.semaphore_wait(barrier, len(partners))
    w_copies = [
        remote(gate_hbm, wgate.at[:, theirs], wsend_sem.at[0], wrecv_sem.at[0], sib),
        remote(up_hbm, wup.at[:, theirs], wsend_sem.at[1], wrecv_sem.at[1], sib),
        remote(down_hbm, wdown.at[theirs, :], wsend_sem.at[2], wrecv_sem.at[2], sib),
    ]

    cut = width // 128 * 3 // 4 * 128
    spans = (pl.ds(0, cut), pl.ds(cut, width - cut))
    LO, HI = 0, 1
    sent = []

    def send_units(half):
        for step in range(1, flight):
            sent.append(
                remote(
                    send_unit.at[step, :, spans[half]],
                    rows.at[flight - step, 0, :, spans[half]],
                    usend_sem.at[step, half],
                    urecv_sem.at[flight - step, half],
                    peer(step),
                )
            )

    def pass_on(e, src, dst, half, target):
        number = 2 * (dst - 1) + half
        sent.append(
            remote(
                rows.at[e, src, :, spans[half]],
                rows.at[e, dst, :, spans[half]],
                nsend_sem.at[e, number],
                rrecv_sem.at[e, number],
                target,
            )
        )

    def got_rows(e, src, half):
        arrived(rows.at[e, src, :, spans[half]], rrecv_sem.at[e, 2 * (src - 1) + half])

    def spread(e, half):
        if half == HI:
            pass_on(e, 0, 1, half, near)
            pass_on(e, 0, 2, half, far)
        else:
            pass_on(e, 0, 2, half, far)
            pass_on(e, 0, 1, half, near)

    def forward(e):
        got_rows(e, 1, HI)
        pass_on(e, 1, 3, HI, far)
        got_rows(e, 2, LO)
        pass_on(e, 2, 3, LO, near)

    def pieces(half):
        low, high = (0, cut) if half == LO else (cut, width)
        step = 6 * 128
        return [pl.ds(at, min(step, high - at)) for at in range(low, high, step)]

    tok_copy.wait()
    for half in (HI, LO):
        for cols in pieces(half):
            got = jnp.dot(hit, tok[:, cols], preferred_element_type=jnp.float32).astype(jnp.bfloat16)
            for step in range(flight):
                unit = got[step * cap : (step + 1) * cap]
                if step == 0:
                    rows[0, 0, :, cols] = unit
                else:
                    send_unit[step, :, cols] = unit
        send_units(half)
        spread(0, half)
    forward(0)
    for half in (HI, LO):
        for e in range(1, flight):
            arrived(rows.at[e, 0, :, spans[half]], urecv_sem.at[e, half])
            spread(e, half)

    def rest(e):
        got_rows(e, 1, LO)
        got_rows(e, 2, HI)
        got_rows(e, 3, HI)
        got_rows(e, 3, LO)

    def hidden(low, high):
        count = (high - low) * 4 * cap
        x = rows[low:high].reshape(count, width)
        gate_val = jnp.dot(x, wgate[...], preferred_element_type=jnp.float32)
        up_val = jnp.dot(x, wup[...], preferred_element_type=jnp.float32)
        return (gate_val / (1.0 + jnp.exp(-gate_val)) * up_val).astype(jnp.bfloat16)

    def send_diag(e, half):
        sent.append(
            remote(
                part_bf.at[e, 3, :, spans[half]],
                diag_in.at[e, :, spans[half]],
                dsend_sem.at[e, half],
                drecv_sem.at[e, half],
                near if half == LO else far,
            )
        )

    def send_sum(e, way, half):
        number = 2 * way + half
        sent.append(
            remote(
                part_bf.at[e, 1 + way, :, spans[half]],
                sums_in.at[e, way, :, spans[half]],
                ssend_sem.at[e, number],
                srecv_sem.at[e, number],
                far if way else near,
            )
        )

    def project(h, low, high):
        for half in (LO, HI):
            for cols in pieces(half):
                val = jnp.dot(h, wdown[:, cols], preferred_element_type=jnp.float32)
                val = val.reshape(high - low, 4, cap, cols.size)
                part[low:high, :, :, cols] = val
                part_bf[low:high, :, :, cols] = val.astype(jnp.bfloat16)
            for e in range(low, high):
                send_diag(e, half)
                send_sum(e, 0 if half == LO else 1, half)

    rest(0)
    for number in range(2):
        own_copies[number].wait()
        w_copies[number].wait_recv()
    hidden_first = hidden(0, 1)
    for e in range(1, flight):
        forward(e)
    own_copies[2].wait()
    w_copies[2].wait_recv()
    project(hidden_first, 0, 1)
    if flight > 1:
        for e in range(1, flight):
            rest(e)
        project(hidden(1, flight), 1, flight)

    for e in range(flight):
        for half, way in ((HI, 0), (LO, 1)):
            cols = spans[half]
            arrived(diag_in.at[e, :, cols], drecv_sem.at[e, half])
            val = part[e, 1 + way, :, cols] + diag_in[e, :, cols].astype(jnp.float32)
            part_bf[e, 1 + way, :, cols] = val.astype(jnp.bfloat16)
            send_sum(e, way, half)

    def total(e, half):
        cols = spans[half]
        for way in range(2):
            arrived(sums_in.at[e, way, :, cols], srecv_sem.at[e, 2 * way + half])
        val = part[e, 0, :, cols] + sums_in[e, 0, :, cols].astype(jnp.float32)
        val = val + sums_in[e, 1, :, cols].astype(jnp.float32)
        return val.astype(jnp.bfloat16)

    for e in range(1, flight):
        for half in (HI, LO):
            cols = spans[half]
            home_out[e, :, cols] = total(e, half)
            sent.append(
                remote(
                    home_out.at[e, :, cols],
                    home_in.at[flight - e, :, cols],
                    hsend_sem.at[e, half],
                    hrecv_sem.at[flight - e, half],
                    peer(e),
                )
            )
    for half in (HI, LO):
        outs_ref[0, :, spans[half]] = total(0, half)
    for step in range(1, flight):
        for half in (HI, LO):
            arrived(home_in.at[step, :, spans[half]], hrecv_sem.at[step, half])
        outs_ref[step] = home_in[step]

    for copy in sent + w_copies:
        copy.wait_send()


def local(
    tokens,
    group_choice,
    expert_picks,
    gate_fixed,
    token_counts,
    expert_gate,
    expert_up,
    expert_down,
):
    flight = lax.axis_size("node") // SPLIT
    token_rows, width = tokens.shape
    cap = token_rows // 16
    hid = expert_gate.shape[1]
    vmem = pl.BlockSpec(memory_space=pltpu.VMEM)
    anywhere = pl.BlockSpec(memory_space=pl.ANY)
    dma = pltpu.SemaphoreType.DMA
    hit, share, outs = pl.pallas_call(
        functools.partial(kernel, flight, cap),
        out_shape=(
            jax.ShapeDtypeStruct((flight * cap, token_rows), jnp.bfloat16),
            jax.ShapeDtypeStruct((1, token_rows), jnp.float32),
            jax.ShapeDtypeStruct((flight, cap, width), jnp.bfloat16),
        ),
        in_specs=[
            anywhere,
            vmem,
            vmem,
            vmem,
            pl.BlockSpec(memory_space=pltpu.SMEM),
            anywhere,
            anywhere,
            anywhere,
        ],
        out_specs=(vmem, vmem, vmem),
        scratch_shapes=[
            pltpu.VMEM((token_rows, width), jnp.bfloat16),
            pltpu.VMEM((width, 2 * hid), jnp.bfloat16),
            pltpu.VMEM((width, 2 * hid), jnp.bfloat16),
            pltpu.VMEM((2 * hid, width), jnp.bfloat16),
            pltpu.VMEM((flight, cap, width), jnp.bfloat16),
            pltpu.VMEM((flight, 4, cap, width), jnp.bfloat16),
            pltpu.VMEM((flight, 4, cap, width), jnp.float32),
            pltpu.VMEM((flight, 4, cap, width), jnp.bfloat16),
            pltpu.VMEM((flight, cap, width), jnp.bfloat16),
            pltpu.VMEM((flight, 2, cap, width), jnp.bfloat16),
            pltpu.VMEM((flight, cap, width), jnp.bfloat16),
            pltpu.VMEM((flight, cap, width), jnp.bfloat16),
            dma(()),
            dma((3,)),
            dma((3,)),
            dma((3,)),
            dma((flight, 2)),
            dma((flight, 2)),
            dma((flight, 6)),
            dma((flight, 6)),
            dma((flight, 2)),
            dma((flight, 2)),
            dma((flight, 4)),
            dma((flight, 4)),
            dma((flight, 2)),
            dma((flight, 2)),
        ],
        compiler_params=pltpu.CompilerParams(
            collective_id=0, has_side_effects=True, vmem_limit_bytes=56 * 1024 * 1024
        ),
    )(tokens, group_choice.T, expert_picks.T, gate_fixed.T, token_counts, expert_gate, expert_up, expert_down)
    back = lax.dot_general(
        hit,
        outs.reshape(flight * cap, width),
        (((0,), (0,)), ((), ())),
        preferred_element_type=jnp.float32,
    )
    return (back * share.reshape(token_rows)[:, None]).astype(tokens.dtype)


def solution(mesh):
    return jax.shard_map(
        local,
        mesh=mesh,
        in_specs=(
            P(("rep", "node"), None),
            P(("rep", "node"), None),
            P(("rep", "node"), None),
            P(("rep", "node"), None),
            P(("rep", "node")),
            P(None, "node"),
            P(None, "node"),
            P("node", None),
        ),
        out_specs=P(("rep", "node"), None),
        check_vma=False,
    )
```
